32 devices in a mesh: seq: 16 (over z, y, core), tensor: 2 (over x).
Axes of the slice: x: 2, y: 2, z: 4, core: 2. Of those that a mesh axis runs over, the one named last changes fastest.
Arguments:
- queries: bfloat16 [4096, 3072], P('seq', 'tensor'), may hold values from -100 to 100
- key_tiles: bfloat16 [4096, 3072], P('seq', 'tensor'), may hold values from -6 to 6
- value_tiles: bfloat16 [4096, 3072], P('seq', 'tensor'), may hold values from -6 to 6
- cache_keys: bfloat16 [32, 128, 3072], P('seq', None, 'tensor'), may hold values from -6 to 6
- cache_values: bfloat16 [32, 128, 3072], P('seq', None, 'tensor'), may hold values from -6 to 6
- hidden: bfloat16 [4096, 5120], P('seq', 'tensor'), may hold values from -6 to 6
- out_weight: bfloat16 [3072, 5120], P('seq', 'tensor'), may hold values from -0.21875 to 0.21875
- gate_table: float32 [1000, 5120], P(None, 'tensor'), may hold values from 0.3 to 2.5
- lengths: int32 [4], replicated, may hold values from 512 to 1536, as said below
- page_table: int32 [4, 4], replicated, may hold values from 0 to 31, as said below
- page_count: int32 [4], replicated, may hold values from 0 to 4
- timestep: int32 [4], replicated, may hold values from 0 to 999
Outputs:
- layer_out: bfloat16 [4096, 5120], P('seq', 'tensor')
The draws below stay inside these ranges and needn't reach their ends.
Inputs may be any that keep to these rules, and one draw needn't show every extreme that they name: The lengths sum to 4096. `page_table`: a page named by clip c lies on a seq index that holds some token of clip c (page p lies on seq index p // 2); a page may be named by several clips or twice.
All inputs are finite; a program needn't handle non-finite values.
Results may differ from the reference program's by a relative error of at most 0.018.
Values may be sent and summed in bfloat16 or wider, within the bound.
A program may use at most 192 MiB of HBM per device.

```python
import math
import jax
import jax.numpy as jnp
from jax import lax

D = 5120
HD = 128
ROWS = 256
LEAST = 512
MOST = 1536
PAGE = 128
POOL = 2
PAGES_CLIP = 4
STEPS = 1000
HQ = 3072
REACH = 6
CLIPS = 4
TOKENS = 4096
N_SEQ = 16


def lengths_helper(key):
    folded = jax.random.fold_in(key, 11)
    first_key, second_key = jax.random.split(folded)
    chosen = jax.random.randint(first_key, (CLIPS // 2,), LEAST, MOST + 1)
    chosen = chosen.at[0].set(MOST)
    paired = jnp.concatenate([chosen, 8 * ROWS - chosen])
    shuffle = jax.random.permutation(second_key, CLIPS)
    return paired[shuffle].astype(jnp.int32)


def draw_lengths(key, part):
    return lengths_helper(key)


def draw_page_table(key, part):
    lengths = lengths_helper(key)
    clip_ends = jnp.cumsum(lengths).astype(jnp.int32)
    clip_starts = clip_ends - lengths
    first_dev = clip_starts // ROWS
    last_dev = (clip_ends - 1) // ROWS
    folded = jax.random.fold_in(key, 12)
    first_key, second_key = jax.random.split(folded)
    offsets = jax.random.randint(first_key, (CLIPS, PAGES_CLIP), 0, 1048576) % (last_dev - first_dev + 1)[:, None]
    owners = first_dev[:, None] + offsets
    slot_ids = jax.random.randint(second_key, (CLIPS, PAGES_CLIP), 0, POOL)
    table = owners * POOL + slot_ids
    column = jnp.arange(PAGES_CLIP)[None, :]
    token_total = 4 * ROWS * CLIPS
    last_page = token_total // ROWS * POOL - 1
    table = jnp.where((clip_ends[:, None] == token_total) & (column == 0), last_page, table)
    table = jnp.where((clip_starts[:, None] == 0) & (column == 1), 0, table)
    return table.astype(jnp.int32)


def draw_page_count(key, part):
    folded = jax.random.fold_in(key, 13)
    counts = jax.random.randint(folded, (CLIPS,), 0, PAGES_CLIP + 1)
    counts = counts.at[0].set(PAGES_CLIP).at[1].set(0)
    return counts.astype(jnp.int32)


def query_key_helper(key):
    folded = jax.random.fold_in(key, 21)
    first_key, second_key = jax.random.split(folded)
    key_draw = jnp.clip(jax.random.normal(first_key, (TOKENS, HQ), jnp.float32), -6.0, 6.0)
    query_draw = 2.0 * jax.random.normal(second_key, (TOKENS, HQ), jnp.float32)
    return (jnp.clip(query_draw, -100.0, 100.0), key_draw)


def draw_queries(key, part):
    return query_key_helper(key)[0].astype(jnp.bfloat16)


def draw_key_tiles(key, part):
    return query_key_helper(key)[1].astype(jnp.bfloat16)


def with_ends(array, key, low, high):
    longest = array.shape.index(max(array.shape))
    spots = []
    for shift in (0, 1):
        where = [jax.random.randint(jax.random.fold_in(key, axis), (), 0, length) for axis, length in enumerate(array.shape)]
        where[longest] = (where[longest] + shift) % array.shape[longest]
        spots.append(tuple(where))
    return array.at[spots[0]].set(low).at[spots[1]].set(high)


def block_scale(stream_key, shape, cuts, smallest, largest):
    gain, own = 1.0, jax.random.fold_in(stream_key, 6)
    for position, parts in cuts:
        heights = jnp.exp(jax.random.uniform(jax.random.fold_in(own, position), (parts,), jnp.float32, smallest / len(cuts), largest / len(cuts)))
        gain = gain * jnp.repeat(heights, shape[position] // parts).reshape([-1 if axis == position else 1 for axis in range(len(shape))])
    return gain


def bell_draw(own_key, extent, scale, most, shards=(), held_as=jnp.bfloat16):
    loudness = block_scale(own_key, extent, shards, -0.22, 0.18) if shards else 1.0
    entries = jax.random.normal(own_key, extent, jnp.float32) * scale * loudness
    return jnp.minimum(jnp.maximum(entries, -most), most).astype(held_as)


def setup_inputs(seed: int = 0) -> dict:
    keys = jax.random.split(jax.random.key(seed), 13)
    return {
        "queries": draw_queries(jax.random.fold_in(keys[12], 71), 0),
        "key_tiles": draw_key_tiles(jax.random.fold_in(keys[12], 71), 0),
        "value_tiles": bell_draw(keys[2], (TOKENS, HQ), 1.0, 6.0, ((0, 16), (1, 2))),
        "cache_keys": bell_draw(keys[3], (N_SEQ * POOL, PAGE, HQ), 1.0, 6.0, ((0, 16), (2, 2))),
        "cache_values": bell_draw(keys[4], (N_SEQ * POOL, PAGE, HQ), 1.0, 6.0, ((0, 16), (2, 2))),
        "hidden": bell_draw(keys[5], (TOKENS, D), 1.0, 6.0, ((0, 16), (1, 2))),
        "out_weight": bell_draw(keys[6], (HQ, D), (HQ // 4) ** -0.5, 0.21875, ((0, 16), (1, 2))),
        "gate_table": jnp.clip(0.3 + 2.2 * jax.random.uniform(keys[7], (STEPS, D), jnp.float32) ** block_scale(keys[7], (STEPS, D), ((1, 2),), -0.2, 0.2), 0.3, 2.5),
        "lengths": draw_lengths(jax.random.fold_in(keys[12], 71), 0),
        "page_table": draw_page_table(jax.random.fold_in(keys[12], 71), 0),
        "page_count": draw_page_count(jax.random.fold_in(keys[12], 71), 0),
        "timestep": with_ends(jax.random.randint(keys[11], (CLIPS,), 0, STEPS), jax.random.fold_in(keys[11], 1), 0, STEPS - 1).astype(jnp.int32),
    }


low_score = -1e+30

def clip_index(positions, clip_ends):
    return lax.optimization_barrier(jnp.sum((positions[:, None] >= clip_ends[None, :]).astype(jnp.int32), axis=1))

def allowed_keys(query_clip, source, clip_ends, page_table, page_count, block_total, row_count):
    key_pos = source * row_count + jnp.arange(row_count, dtype=jnp.int32)
    in_range = (source >= 0) & (source < block_total)
    same_clip = (query_clip[:, None] == clip_index(key_pos, clip_ends)[None, :]) & in_range
    clip_total = clip_ends.shape[0]
    page_ids = source * POOL + jnp.arange(POOL, dtype=jnp.int32)
    live_slots = jnp.arange(page_table.shape[1], dtype=jnp.int32)[None, :] < page_count[:, None]
    named_pages = jnp.any(live_slots[:, :, None] & (page_table[:, :, None] == page_ids[None, None, :]), axis=1)
    member = query_clip[:, None] == jnp.arange(clip_total, dtype=jnp.int32)[None, :]
    page_ok = jnp.any(member[:, :, None] & named_pages[None], axis=1) & in_range
    page_ok = jnp.repeat(page_ok, PAGE, axis=1)
    return jnp.concatenate([same_clip, page_ok], axis=1)

def reference(queries, key_tiles, value_tiles, cache_keys, cache_values, hidden, out_weight, gate_table, lengths, page_table, page_count, timestep):
    token_total = queries.shape[0]
    tile_width = queries.shape[1]
    head_count = tile_width // HD
    block_total = token_total // ROWS
    clip_ends = jnp.cumsum(lengths, dtype=jnp.int32)
    packed_keys = jnp.concatenate([key_tiles.reshape(block_total, ROWS, tile_width), cache_keys.reshape(block_total, POOL * PAGE, tile_width)], axis=1)
    packed_values = jnp.concatenate([value_tiles.reshape(block_total, ROWS, tile_width), cache_values.reshape(block_total, POOL * PAGE, tile_width)], axis=1)
    padded_keys = jnp.pad(packed_keys, ((REACH, REACH), (0, 0), (0, 0)))
    padded_values = jnp.pad(packed_values, ((REACH, REACH), (0, 0), (0, 0)))
    inv_root = 1.0 / math.sqrt(HD)

    def one_block(block_id):
        block_id = block_id.astype(jnp.int32)
        positions = block_id * ROWS + jnp.arange(ROWS, dtype=jnp.int32)
        query_clip = clip_index(positions, clip_ends)
        window_keys = lax.dynamic_slice_in_dim(padded_keys, block_id, 2 * REACH + 1, 0).reshape(-1, head_count, HD)
        window_values = lax.dynamic_slice_in_dim(padded_values, block_id, 2 * REACH + 1, 0).reshape(-1, head_count, HD)
        masks = [allowed_keys(query_clip, block_id - REACH + offset, clip_ends, page_table, page_count, block_total, ROWS) for offset in range(2 * REACH + 1)]
        allowed = jnp.concatenate(masks, axis=1)
        query_rows = lax.dynamic_slice_in_dim(queries, block_id * ROWS, ROWS, 0).reshape(ROWS, head_count, HD)
        scores = jnp.einsum('qhd,khd->hqk', query_rows.astype(jnp.float32), window_keys.astype(jnp.float32)) * inv_root
        scores = jnp.where(allowed[None], scores, low_score)
        top_score = lax.optimization_barrier(jnp.max(scores, axis=2))
        weights = jnp.where(allowed[None], jnp.exp(scores - top_score[:, :, None]), 0.0)
        totals = lax.optimization_barrier(jnp.sum(weights, axis=2))
        rounded = weights.astype(jnp.bfloat16)
        summed = jnp.einsum('hqk,khd->hqd', rounded.astype(jnp.float32), window_values.astype(jnp.float32))
        result = summed / totals[:, :, None]
        return jnp.transpose(result, (1, 0, 2)).reshape(ROWS, tile_width).astype(jnp.bfloat16)
    attention = lax.map(one_block, jnp.arange(block_total, dtype=jnp.int32)).reshape(token_total, tile_width)
    projected = jnp.dot(attention, out_weight, preferred_element_type=jnp.float32)
    token_clip = clip_index(jnp.arange(token_total, dtype=jnp.int32), clip_ends)
    token_gate = gate_table[timestep[token_clip]]
    return (hidden.astype(jnp.float32) + token_gate * projected).astype(jnp.bfloat16)
```

```python
import functools
import math

import jax
import jax.numpy as jnp
from jax import lax
from jax.experimental import pallas as pl
from jax.experimental.pallas import tpu as pltpu
from jax.sharding import PartitionSpec as P

HD = 128
PAGE = 128
POOL = 2
REACH = 6

MESH = pl.DeviceIdType.MESH
ANY = pl.BlockSpec(memory_space=pl.ANY)
VMEM = pl.BlockSpec(memory_space=pltpu.VMEM)
SMEM = pl.BlockSpec(memory_space=pltpu.SMEM)
SCALE = math.log2(math.e) / math.sqrt(HD)


def owner_of(head, heads, n):
    return lax.div(head * n, heads)


def owned_by(index, heads, n):
    head = lax.div(index * heads + n - 1, n)
    return (head < heads) & (owner_of(head, heads, n) == index), head


def greet_seq(n, me, tensor):
    barrier = pltpu.get_barrier_semaphore()

    def signal(step, carry):
        peer = (me + step) % n
        pl.semaphore_signal(barrier, inc=1, device_id=(peer, tensor), device_id_type=MESH)
        return carry

    lax.fori_loop(1, n, signal, 0)
    return barrier


def scatter_heads(n, heads, q, k, v, ck, cv, out, send_sem, recv_sem):
    me, tensor = lax.axis_index("seq"), lax.axis_index("tensor")
    barrier = greet_seq(n, me, tensor)
    pl.semaphore_wait(barrier, n - 1)
    mine, _ = owned_by(me, heads, n)

    def send(step, carry):
        head = (step + me) % heads
        owner = owner_of(head, heads, n)
        columns = pl.ds(pl.multiple_of(head * HD, HD), HD)

        @pl.when(owner == me)
        def _():
            for a, ref in enumerate((q, k, v, ck, cv)):
                pltpu.make_async_copy(ref.at[:, columns], out.at[a, me], recv_sem.at[a]).start()

        @pl.when(owner != me)
        def _():
            for a, ref in enumerate((q, k, v, ck, cv)):
                pltpu.make_async_remote_copy(
                    src_ref=ref.at[:, columns],
                    dst_ref=out.at[a, me],
                    send_sem=send_sem.at[a],
                    recv_sem=recv_sem.at[a],
                    device_id=(owner, tensor),
                    device_id_type=MESH,
                ).start()

        return carry

    lax.fori_loop(0, heads, send, 0)

    @pl.when(mine)
    def _():
        for a, ref in enumerate((q, k, v, ck, cv)):
            pltpu.make_async_copy(out.at[a], out.at[a], recv_sem.at[a]).wait()
            if heads > 1:
                part = ref.at[:, pl.ds(0, (heads - 1) * HD)]
                pltpu.make_async_copy(part, part, send_sem.at[a]).wait()

    @pl.when(jnp.logical_not(mine))
    def _():
        for a, ref in enumerate((q, k, v, ck, cv)):
            pltpu.make_async_copy(ref, ref, send_sem.at[a]).wait()


def attend_head(n, heads, rows, window, clips, slots, lengths, page_table, page_count, r, out, scores):
    contract = (((1,), (1,)), ((), ()))

    def item(c, block, start, end, base, token_blocks, page_pairs):
        query = r[0, block]
        chunks = []
        for j in range(token_blocks):
            position = (base + j) * rows + lax.broadcasted_iota(jnp.int32, (1, rows), 1)
            ok = (position >= start) & (position < end)
            chunks.append((r[1, base + j], r[2, base + j], ok))
        count = page_count[c]
        lane = lax.broadcasted_iota(jnp.int32, (1, 2 * PAGE), 1)
        for pair in range(page_pairs):
            keys, values, live = [], [], []
            for slot in (2 * pair, 2 * pair + 1):
                real = min(slot, slots - 1)
                page = page_table[c, real]
                alive = jnp.int32(slot) < count
                if slot >= slots:
                    alive = alive & False
                for before in range(real):
                    alive = alive & (page_table[c, before] != page)
                owner = page // POOL
                offset = pl.ds(pl.multiple_of((page % POOL) * PAGE, PAGE), PAGE)
                keys.append(r[3, owner, offset])
                values.append(r[4, owner, offset])
                live.append(alive.astype(jnp.int32))
            ok = jnp.where(lane < PAGE, live[0], live[1]) > 0
            chunks.append(
                (jnp.concatenate(keys, axis=0), jnp.concatenate(values, axis=0), ok)
            )
        top = None
        width = chunks[0][0].shape[0]
        for j, (key, _, ok) in enumerate(chunks):
            s = lax.dot_general(query, key, contract, preferred_element_type=jnp.float32)
            s = s * SCALE + jnp.where(ok, 0.0, -1e30)
            scores[:, j * width : (j + 1) * width] = s
            part = jnp.maximum(s[:, :HD], s[:, HD:])
            top = part if top is None else jnp.maximum(top, part)
        top = jnp.max(top, axis=1, keepdims=True)
        total = None
        for j, (_, value, _) in enumerate(chunks):
            weight = jnp.exp2(scores[:, j * width : (j + 1) * width] - top).astype(jnp.bfloat16)
            wide = jnp.concatenate([value, jnp.ones_like(value)], axis=1)
            add = jnp.dot(weight, wide, preferred_element_type=jnp.float32)
            total = add if total is None else total + add
        result = (total[:, :HD] / total[:, HD:]).astype(jnp.bfloat16)
        position = block * rows + lax.broadcasted_iota(jnp.int32, (rows, HD), 0)
        inside = (position >= start) & (position < end)
        out[block] = jnp.where(inside, result, out[block])

    mine, _ = owned_by(lax.axis_index("seq"), heads, n)

    @pl.when(mine)
    def _():
        def clip_step(c, start):
            end = start + lengths[c]
            first = start // rows
            last = (end - 1) // rows
            span = last - first + 1
            count = page_count[c]
            pairs = (slots + 1) // 2
            small = min((window + 1) // 2, window)

            def run(token_blocks, page_pairs):
                base = jnp.minimum(first, n - token_blocks)

                def step(block, carry):
                    item(c, block, start, end, base, token_blocks, page_pairs)
                    return carry

                lax.fori_loop(first, last + 1, step, 0)

            for token_blocks, fits in ((small, span <= small), (window, span > small)):
                for page_pairs, named in ((0, count <= 0), (pairs, count > 0)):
                    pl.when(fits & named)(functools.partial(run, token_blocks, page_pairs))
            return end

        lax.fori_loop(0, clips, clip_step, jnp.int32(0))


def return_heads(n, tensors, heads, att, out, send_sem, recv_sem, pass_sem, land_sem):
    me, tensor = lax.axis_index("seq"), lax.axis_index("tensor")
    barrier = greet_seq(n, me, tensor)

    def greet(step, carry):
        peer = (tensor + step) % tensors
        pl.semaphore_signal(barrier, inc=1, device_id=(me, peer), device_id_type=MESH)
        return carry

    lax.fori_loop(1, tensors, greet, 0)
    pl.semaphore_wait(barrier, n - 1 + tensors - 1)
    mine, my_head = owned_by(me, heads, n)

    def place(head, side):
        return out.at[:, pl.ds(pl.multiple_of((side * heads + head) * HD, HD), HD)]

    @pl.when(mine)
    def _():
        def send(step, carry):
            peer = (me + step) % n
            pltpu.make_async_remote_copy(
                src_ref=att.at[peer],
                dst_ref=place(my_head, tensor),
                send_sem=send_sem.at[0],
                recv_sem=recv_sem.at[my_head],
                device_id=(peer, tensor),
                device_id_type=MESH,
            ).start()
            return carry

        lax.fori_loop(1, n, send, 0)
        pltpu.make_async_copy(att.at[me], place(my_head, tensor), recv_sem.at[my_head]).start()

    def relay(step, carry):
        head = step
        here = place(head, tensor)
        pltpu.make_async_copy(here, here, recv_sem.at[head]).wait()

        def pass_on(other, inner):
            peer = (tensor + other) % tensors
            pltpu.make_async_remote_copy(
                src_ref=here,
                dst_ref=here,
                send_sem=pass_sem.at[head],
                recv_sem=land_sem.at[tensor, head],
                device_id=(me, peer),
                device_id_type=MESH,
            ).start()
            return inner

        lax.fori_loop(1, tensors, pass_on, 0)
        return carry

    lax.fori_loop(0, heads, relay, 0)

    def finish(step, carry):
        def land(other, inner):
            peer = (tensor + other) % tensors
            there = place(step, peer)
            pltpu.make_async_copy(there, there, land_sem.at[peer, step]).wait()
            mine_here = place(step, tensor)
            pltpu.make_async_copy(mine_here, mine_here, pass_sem.at[step]).wait()
            return inner

        return lax.fori_loop(1, tensors, land, carry)

    lax.fori_loop(0, heads, finish, 0)

    @pl.when(mine)
    def _():
        part = att.at[pl.ds(0, n - 1)]
        pltpu.make_async_copy(part, part, send_sem.at[0]).wait()


def clip_index(positions, clip_ends):
    return jnp.sum((positions[:, None] >= clip_ends[None, :]).astype(jnp.int32), axis=1)


def local(
    n,
    tensors,
    queries,
    key_tiles,
    value_tiles,
    cache_keys,
    cache_values,
    hidden,
    out_weight,
    gate_table,
    lengths,
    page_table,
    page_count,
    timestep,
):
    rows, tile_width = queries.shape
    heads = tile_width // HD
    clips, slots = page_table.shape
    seq_index = lax.axis_index("seq")
    window = min(REACH + 1, n)
    pairs = (slots + 1) // 2

    weight = lax.all_gather(out_weight, "seq", axis=0, tiled=True)

    received = pl.pallas_call(
        functools.partial(scatter_heads, n, heads),
        out_shape=jax.ShapeDtypeStruct((5, n, rows, HD), jnp.bfloat16),
        in_specs=[ANY] * 5,
        out_specs=ANY,
        scratch_shapes=[pltpu.SemaphoreType.DMA((5,)), pltpu.SemaphoreType.DMA((5,))],
        compiler_params=pltpu.CompilerParams(collective_id=0, has_side_effects=True),
        cost_estimate=pl.CostEstimate(flops=0, bytes_accessed=200_000_000, transcendentals=0),
        name="scatter_heads",
    )(
        queries,
        key_tiles,
        value_tiles,
        cache_keys.reshape(rows, tile_width),
        cache_values.reshape(rows, tile_width),
    )

    attended = pl.pallas_call(
        functools.partial(attend_head, n, heads, rows, window, clips, slots),
        out_shape=jax.ShapeDtypeStruct((n, rows, HD), jnp.bfloat16),
        in_specs=[SMEM] * 3 + [VMEM],
        out_specs=VMEM,
        scratch_shapes=[pltpu.VMEM((rows, (window + pairs) * rows), jnp.float32)],
        compiler_params=pltpu.CompilerParams(vmem_limit_bytes=50 * 1024 * 1024),
        cost_estimate=pl.CostEstimate(
            flops=4 * n * rows * window * rows * HD,
            bytes_accessed=6 * n * rows * HD * 2,
            transcendentals=n * rows * window * rows,
        ),
        name="attend_head",
    )(lengths, page_table, page_count, received)

    attention = pl.pallas_call(
        functools.partial(return_heads, n, tensors, heads),
        out_shape=jax.ShapeDtypeStruct((rows, tensors * tile_width), jnp.bfloat16),
        in_specs=[ANY],
        out_specs=ANY,
        scratch_shapes=[
            pltpu.SemaphoreType.DMA((1,)),
            pltpu.SemaphoreType.DMA((heads,)),
            pltpu.SemaphoreType.DMA((heads,)),
            pltpu.SemaphoreType.DMA((tensors, heads)),
        ],
        compiler_params=pltpu.CompilerParams(collective_id=1, has_side_effects=True),
        cost_estimate=pl.CostEstimate(flops=0, bytes_accessed=80_000_000, transcendentals=0),
        name="return_heads",
    )(attended)

    projected = jnp.dot(attention, weight, preferred_element_type=jnp.float32)
    clip_ends = jnp.cumsum(lengths, dtype=jnp.int32)
    positions = seq_index * rows + jnp.arange(rows, dtype=jnp.int32)
    query_clip = clip_index(positions, clip_ends)
    gates = [
        lax.dynamic_slice_in_dim(gate_table, timestep[c], 1, 0) for c in range(clips)
    ]
    token_gate = gates[0]
    for c in range(1, clips):
        token_gate = jnp.where(query_clip[:, None] == c, gates[c], token_gate)
    return (hidden.astype(jnp.float32) + token_gate * projected).astype(jnp.bfloat16)


def solution(mesh):
    return jax.shard_map(
        functools.partial(local, mesh.shape["seq"], mesh.shape["tensor"]),
        mesh=mesh,
        in_specs=(
            P("seq", "tensor"),
            P("seq", "tensor"),
            P("seq", "tensor"),
            P("seq", None, "tensor"),
            P("seq", None, "tensor"),
            P("seq", "tensor"),
            P("seq", "tensor"),
            P(None, "tensor"),
            P(),
            P(),
            P(),
            P(),
        ),
        out_specs=P("seq", "tensor"),
        check_vma=False,
    )
```

```python
import functools
import math

import jax
import jax.numpy as jnp
from jax import lax
from jax.experimental import pallas as pl
from jax.experimental.pallas import tpu as pltpu
from jax.sharding import PartitionSpec as P

HD = 128
PAGE = 128
POOL = 2
REACH = 6

MESH = pl.DeviceIdType.MESH
ANY = pl.BlockSpec(memory_space=pl.ANY)
VMEM = pl.BlockSpec(memory_space=pltpu.VMEM)
SMEM = pl.BlockSpec(memory_space=pltpu.SMEM)
SCALE = math.log2(math.e) / math.sqrt(HD)


def owner_of(head, heads, n):
    return lax.div(head * n, heads)


def owned_by(index, heads, n):
    head = lax.div(index * heads + n - 1, n)
    return (head < heads) & (owner_of(head, heads, n) == index), head


def inner_chips(n):
    inner = 1
    while (2 * inner) ** 2 <= n // 2:
        inner *= 2
    return inner


def greet_seq(n, me, tensor):
    barrier = pltpu.get_barrier_semaphore()

    def signal(step, carry):
        peer = (me + step) % n
        pl.semaphore_signal(barrier, inc=1, device_id=(peer, tensor), device_id_type=MESH)
        return carry

    lax.fori_loop(1, n, signal, 0)
    return barrier


def scatter_heads(
    n, heads, wide, q, k, v, ck, cv, w, out, w_out, send_sem, recv_sem, w_send, w_recv
):
    me, tensor = lax.axis_index("seq"), lax.axis_index("tensor")
    inner = inner_chips(n)
    outer = n // 2 // inner
    a, b, c = lax.div(me, 2 * inner), lax.rem(lax.div(me, 2), inner), lax.rem(me, 2)
    w_rows = w.shape[0]
    own = w.at[:, pl.ds(0, wide)]
    barrier = greet_seq(n, me, tensor)
    pl.semaphore_wait(barrier, n - 1)
    mine, _ = owned_by(me, heads, n)

    def index(a_at, b_at, c_at):
        return (a_at * inner + b_at) * 2 + c_at

    def slot(i):
        return w_out.at[pl.ds(pl.multiple_of(i * w_rows, w_rows), w_rows)]

    def pass_block(src, i, kind, target):
        pltpu.make_async_remote_copy(
            src_ref=src,
            dst_ref=slot(i),
            send_sem=w_send.at[kind, i],
            recv_sem=w_recv.at[i],
            device_id=(target, tensor),
            device_id_type=MESH,
        ).start()

    def arrived(i):
        pltpu.make_async_copy(slot(i), slot(i), w_recv.at[i]).wait()

    def along_outer(src, i, up, down):
        if up:
            pl.when(a + 1 < outer)(lambda: pass_block(src, i, 0, index(a + 1, b, c)))
        if down:
            pl.when(a > 0)(lambda: pass_block(src, i, 1, index(a - 1, b, c)))

    def along_inner(src, i, up, down):
        if up:
            pl.when(b + 1 < inner)(lambda: pass_block(src, i, 2, index(a, b + 1, c)))
        if down:
            pl.when(b > 0)(lambda: pass_block(src, i, 3, index(a, b - 1, c)))

    def across(src, i):
        pass_block(src, i, 4, index(a, b, 1 - c))

    along_outer(own, me, True, True)
    along_inner(own, me, True, True)
    across(own, me)
    pltpu.make_async_copy(own, slot(me), w_recv.at[me]).start()

    def send(step, carry):
        head = lax.rem(step + me, heads)
        owner = owner_of(head, heads, n)
        columns = pl.ds(pl.multiple_of(head * HD, HD), HD)

        @pl.when(owner == me)
        def _():
            for i, ref in enumerate((q, k, v, ck, cv)):
                pltpu.make_async_copy(ref.at[:, columns], out.at[i, me], recv_sem.at[i]).start()

        @pl.when(owner != me)
        def _():
            for i, ref in enumerate((q, k, v, ck, cv)):
                pltpu.make_async_remote_copy(
                    src_ref=ref.at[:, columns],
                    dst_ref=out.at[i, me],
                    send_sem=send_sem.at[i],
                    recv_sem=recv_sem.at[i],
                    device_id=(owner, tensor),
                    device_id_type=MESH,
                ).start()

        return carry

    stages = [heads // 2 + (heads - heads // 2) * d // (outer - 1) for d in range(outer)]
    lax.fori_loop(0, stages[0], send, 0)
    for d in range(1, outer):

        @pl.when(a - d >= 0)
        def _():
            i = index(a - d, b, c)
            arrived(i)
            along_outer(slot(i), i, True, False)
            along_inner(slot(i), i, True, True)
            across(slot(i), i)

        @pl.when(a + d < outer)
        def _():
            i = index(a + d, b, c)
            arrived(i)
            along_outer(slot(i), i, False, True)
            along_inner(slot(i), i, True, True)
            across(slot(i), i)

        lax.fori_loop(stages[d - 1], stages[d], send, 0)

    for e in range(1, inner):

        def inner_step(step, carry):
            a_at = lax.rem(a + step, outer)

            @pl.when(b - e >= 0)
            def _():
                i = index(a_at, b - e, c)
                arrived(i)
                along_inner(slot(i), i, True, False)
                across(slot(i), i)

            @pl.when(b + e < inner)
            def _():
                i = index(a_at, b + e, c)
                arrived(i)
                along_inner(slot(i), i, False, True)
                across(slot(i), i)

            return carry

        lax.fori_loop(0, outer, inner_step, 0)

    def sibling_step(chip, carry):
        arrived(chip * 2 + (1 - c))
        return carry

    lax.fori_loop(0, n // 2, sibling_step, 0)
    arrived(me)

    def sent_step(chip, carry):
        i = chip * 2 + c
        a_at, b_at = lax.div(chip, inner), lax.rem(chip, inner)

        def sent(kind):
            pltpu.make_async_copy(slot(i), slot(i), w_send.at[kind, i]).wait()

        pl.when((b_at == b) & (a_at <= a) & (a + 1 < outer))(lambda: sent(0))
        pl.when((b_at == b) & (a_at >= a) & (a > 0))(lambda: sent(1))
        pl.when((b_at <= b) & (b + 1 < inner))(lambda: sent(2))
        pl.when((b_at >= b) & (b > 0))(lambda: sent(3))
        sent(4)
        return carry

    lax.fori_loop(0, n // 2, sent_step, 0)

    @pl.when(mine)
    def _():
        for i, ref in enumerate((q, k, v, ck, cv)):
            pltpu.make_async_copy(out.at[i], out.at[i], recv_sem.at[i]).wait()
            if heads > 1:
                part = ref.at[:, pl.ds(0, (heads - 1) * HD)]
                pltpu.make_async_copy(part, part, send_sem.at[i]).wait()

    @pl.when(jnp.logical_not(mine))
    def _():
        for i, ref in enumerate((q, k, v, ck, cv)):
            pltpu.make_async_copy(ref, ref, send_sem.at[i]).wait()


def attend_head(n, heads, rows, window, clips, slots, lengths, page_table, page_count, r, out, scores):
    contract = (((1,), (1,)), ((), ()))

    def item(c, block, start, end, base, token_blocks, page_pairs):
        query = r[0, block]
        chunks = []
        for j in range(token_blocks):
            position = (base + j) * rows + lax.broadcasted_iota(jnp.int32, (1, rows), 1)
            ok = (position >= start) & (position < end)
            chunks.append((r[1, base + j], r[2, base + j], ok))
        count = page_count[c]
        lane = lax.broadcasted_iota(jnp.int32, (1, 2 * PAGE), 1)
        for pair in range(page_pairs):
            keys, values, live = [], [], []
            for slot in (2 * pair, 2 * pair + 1):
                real = min(slot, slots - 1)
                page = page_table[c, real]
                alive = jnp.int32(slot) < count
                if slot >= slots:
                    alive = alive & False
                for before in range(real):
                    alive = alive & (page_table[c, before] != page)
                owner = page // POOL
                offset = pl.ds(pl.multiple_of((page % POOL) * PAGE, PAGE), PAGE)
                keys.append(r[3, owner, offset])
                values.append(r[4, owner, offset])
                live.append(alive.astype(jnp.int32))
            ok = jnp.where(lane < PAGE, live[0], live[1]) > 0
            chunks.append(
                (jnp.concatenate(keys, axis=0), jnp.concatenate(values, axis=0), ok)
            )
        top = None
        width = chunks[0][0].shape[0]
        for j, (key, _, ok) in enumerate(chunks):
            s = lax.dot_general(query, key, contract, preferred_element_type=jnp.float32)
            s = s * SCALE + jnp.where(ok, 0.0, -1e30)
            scores[:, j * width : (j + 1) * width] = s
            part = jnp.maximum(s[:, :HD], s[:, HD:])
            top = part if top is None else jnp.maximum(top, part)
        top = jnp.max(top, axis=1, keepdims=True)
        total = None
        for j, (_, value, _) in enumerate(chunks):
            weight = jnp.exp2(scores[:, j * width : (j + 1) * width] - top).astype(jnp.bfloat16)
            wide = jnp.concatenate([value, jnp.ones_like(value)], axis=1)
            add = jnp.dot(weight, wide, preferred_element_type=jnp.float32)
            total = add if total is None else total + add
        result = (total[:, :HD] / total[:, HD:]).astype(jnp.bfloat16)
        position = block * rows + lax.broadcasted_iota(jnp.int32, (rows, HD), 0)
        inside = (position >= start) & (position < end)
        out[block] = jnp.where(inside, result, out[block])

    mine, _ = owned_by(lax.axis_index("seq"), heads, n)

    @pl.when(mine)
    def _():
        def clip_step(c, start):
            end = start + lengths[c]
            first = start // rows
            last = (end - 1) // rows
            span = last - first + 1
            count = page_count[c]
            pairs = (slots + 1) // 2
            small = min((window + 1) // 2, window)

            def run(token_blocks, page_pairs):
                base = jnp.minimum(first, n - token_blocks)

                def step(block, carry):
                    item(c, block, start, end, base, token_blocks, page_pairs)
                    return carry

                lax.fori_loop(first, last + 1, step, 0)

            for token_blocks, fits in ((small, span <= small), (window, span > small)):
                for page_pairs, named in ((0, count <= 0), (pairs, count > 0)):
                    pl.when(fits & named)(functools.partial(run, token_blocks, page_pairs))
            return end

        lax.fori_loop(0, clips, clip_step, jnp.int32(0))


def return_heads(n, tensors, heads, att, out, send_sem, recv_sem, pass_sem, land_sem):
    me, tensor = lax.axis_index("seq"), lax.axis_index("tensor")
    barrier = greet_seq(n, me, tensor)

    def greet(step, carry):
        peer = (tensor + step) % tensors
        pl.semaphore_signal(barrier, inc=1, device_id=(me, peer), device_id_type=MESH)
        return carry

    lax.fori_loop(1, tensors, greet, 0)
    pl.semaphore_wait(barrier, n - 1 + tensors - 1)
    mine, my_head = owned_by(me, heads, n)

    def place(head, side):
        return out.at[:, pl.ds(pl.multiple_of((side * heads + head) * HD, HD), HD)]

    @pl.when(mine)
    def _():
        def send(step, carry):
            peer = (me + step) % n
            pltpu.make_async_remote_copy(
                src_ref=att.at[peer],
                dst_ref=place(my_head, tensor),
                send_sem=send_sem.at[0],
                recv_sem=recv_sem.at[my_head],
                device_id=(peer, tensor),
                device_id_type=MESH,
            ).start()
            return carry

        lax.fori_loop(1, n, send, 0)
        pltpu.make_async_copy(att.at[me], place(my_head, tensor), recv_sem.at[my_head]).start()

    def relay(step, carry):
        head = step
        here = place(head, tensor)
        pltpu.make_async_copy(here, here, recv_sem.at[head]).wait()

        def pass_on(other, inner):
            peer = (tensor + other) % tensors
            pltpu.make_async_remote_copy(
                src_ref=here,
                dst_ref=here,
                send_sem=pass_sem.at[head],
                recv_sem=land_sem.at[tensor, head],
                device_id=(me, peer),
                device_id_type=MESH,
            ).start()
            return inner

        lax.fori_loop(1, tensors, pass_on, 0)
        return carry

    lax.fori_loop(0, heads, relay, 0)

    def finish(step, carry):
        def land(other, inner):
            peer = (tensor + other) % tensors
            there = place(step, peer)
            pltpu.make_async_copy(there, there, land_sem.at[peer, step]).wait()
            mine_here = place(step, tensor)
            pltpu.make_async_copy(mine_here, mine_here, pass_sem.at[step]).wait()
            return inner

        return lax.fori_loop(1, tensors, land, carry)

    lax.fori_loop(0, heads, finish, 0)

    @pl.when(mine)
    def _():
        part = att.at[pl.ds(0, n - 1)]
        pltpu.make_async_copy(part, part, send_sem.at[0]).wait()


def project_rows(
    clips, rows, first_tiles, lengths, timestep, attention, w_first, w_rest, hidden, *refs
):
    gates, out = refs[:clips], refs[clips]
    tile = pl.program_id(0)
    position = lax.axis_index("seq") * rows + lax.broadcasted_iota(jnp.int32, out.shape, 0)
    gate, end = None, jnp.int32(0)
    for c in range(clips):
        row = gates[c][pl.ds(lax.rem(timestep[c], 8), 1), :]
        gate = jnp.broadcast_to(row, out.shape) if gate is None else jnp.where(position >= end, row, gate)
        end = end + lengths[c]

    def finish(weight):
        projected = jnp.dot(attention[...], weight[...], preferred_element_type=jnp.float32)
        out[...] = (hidden[...].astype(jnp.float32) + gate * projected).astype(out.dtype)

    pl.when(tile < first_tiles)(lambda: finish(w_first))
    pl.when(tile >= first_tiles)(lambda: finish(w_rest))


def local(
    n,
    tensors,
    queries,
    key_tiles,
    value_tiles,
    cache_keys,
    cache_values,
    hidden,
    out_weight,
    gate_table,
    lengths,
    page_table,
    page_count,
    timestep,
):
    rows, tile_width = queries.shape
    heads = tile_width // HD
    clips, slots = page_table.shape
    window = min(REACH + 1, n)
    pairs = (slots + 1) // 2

    width = out_weight.shape[1]
    tile = 256 if width % 256 == 0 else 128
    first_tiles = (7 * (width // tile) + 5) // 10
    wide = first_tiles * tile

    received, w_first = pl.pallas_call(
        functools.partial(scatter_heads, n, heads, wide),
        out_shape=(
            jax.ShapeDtypeStruct((5, n, rows, HD), jnp.bfloat16),
            jax.ShapeDtypeStruct((n * out_weight.shape[0], wide), jnp.bfloat16),
        ),
        in_specs=[ANY] * 6,
        out_specs=(ANY, ANY),
        scratch_shapes=[
            pltpu.SemaphoreType.DMA((5,)),
            pltpu.SemaphoreType.DMA((5,)),
            pltpu.SemaphoreType.DMA((5, n)),
            pltpu.SemaphoreType.DMA((n,)),
        ],
        compiler_params=pltpu.CompilerParams(collective_id=0, has_side_effects=True),
        cost_estimate=pl.CostEstimate(flops=0, bytes_accessed=300_000_000, transcendentals=0),
        name="scatter_heads",
    )(
        queries,
        key_tiles,
        value_tiles,
        cache_keys.reshape(rows, tile_width),
        cache_values.reshape(rows, tile_width),
        out_weight,
    )
    rest, received = lax.optimization_barrier((out_weight[:, wide:], received))
    w_rest = lax.all_gather(rest, "seq", axis=0, tiled=True)

    attended = pl.pallas_call(
        functools.partial(attend_head, n, heads, rows, window, clips, slots),
        out_shape=jax.ShapeDtypeStruct((n, rows, HD), jnp.bfloat16),
        in_specs=[SMEM] * 3 + [VMEM],
        out_specs=VMEM,
        scratch_shapes=[pltpu.VMEM((rows, (window + pairs) * rows), jnp.float32)],
        compiler_params=pltpu.CompilerParams(vmem_limit_bytes=56 * 1024 * 1024),
        cost_estimate=pl.CostEstimate(
            flops=4 * n * rows * window * rows * HD,
            bytes_accessed=6 * n * rows * HD * 2,
            transcendentals=n * rows * window * rows,
        ),
        name="attend_head",
    )(lengths, page_table, page_count, received)

    attention = pl.pallas_call(
        functools.partial(return_heads, n, tensors, heads),
        out_shape=jax.ShapeDtypeStruct((rows, tensors * tile_width), jnp.bfloat16),
        in_specs=[ANY],
        out_specs=ANY,
        scratch_shapes=[
            pltpu.SemaphoreType.DMA((1,)),
            pltpu.SemaphoreType.DMA((heads,)),
            pltpu.SemaphoreType.DMA((heads,)),
            pltpu.SemaphoreType.DMA((tensors, heads)),
        ],
        compiler_params=pltpu.CompilerParams(collective_id=1, has_side_effects=True),
        cost_estimate=pl.CostEstimate(flops=0, bytes_accessed=80_000_000, transcendentals=0),
        name="return_heads",
    )(attended)

    features = n * out_weight.shape[0]
    gate_specs = [
        pl.BlockSpec((8, tile), lambda j, lengths, timestep, c=c: (lax.div(timestep[c], 8), j))
        for c in range(clips)
    ]
    return pl.pallas_call(
        functools.partial(project_rows, clips, rows, first_tiles),
        out_shape=jax.ShapeDtypeStruct(hidden.shape, hidden.dtype),
        grid_spec=pltpu.PrefetchScalarGridSpec(
            num_scalar_prefetch=2,
            grid=(width // tile,),
            in_specs=[
                pl.BlockSpec((rows, features), lambda j, *_: (0, 0)),
                pl.BlockSpec((features, tile), lambda j, *_: (0, jnp.minimum(j, first_tiles - 1))),
                pl.BlockSpec((features, tile), lambda j, *_: (0, jnp.maximum(j - first_tiles, 0))),
                pl.BlockSpec((rows, tile), lambda j, *_: (0, j)),
                *gate_specs,
            ],
            out_specs=pl.BlockSpec((rows, tile), lambda j, *_: (0, j)),
        ),
        compiler_params=pltpu.CompilerParams(vmem_limit_bytes=56 * 1024 * 1024),
        cost_estimate=pl.CostEstimate(
            flops=2 * rows * features * width,
            bytes_accessed=2 * features * width,
            transcendentals=0,
        ),
        name="project_rows",
    )(lengths, timestep, attention, w_first, w_rest, hidden, *([gate_table] * clips))


def solution(mesh):
    return jax.shard_map(
        functools.partial(local, mesh.shape["seq"], mesh.shape["tensor"]),
        mesh=mesh,
        in_specs=(
            P("seq", "tensor"),
            P("seq", "tensor"),
            P("seq", "tensor"),
            P("seq", None, "tensor"),
            P("seq", None, "tensor"),
            P("seq", "tensor"),
            P("seq", "tensor"),
            P(None, "tensor"),
            P(),
            P(),
            P(),
            P(),
        ),
        out_specs=P("seq", "tensor"),
        check_vma=False,
    )
```

```python
import functools
import math

import jax
import jax.numpy as jnp
from jax import lax
from jax.experimental import pallas as pl
from jax.experimental.pallas import tpu as pltpu
from jax.sharding import PartitionSpec as P

HD = 128
PAGE = 128
POOL = 2
REACH = 6
CHUNKS = 3

MESH = pl.DeviceIdType.MESH
ANY = pl.BlockSpec(memory_space=pl.ANY)
VMEM = pl.BlockSpec(memory_space=pltpu.VMEM)
SMEM = pl.BlockSpec(memory_space=pltpu.SMEM)
SCALE = math.log2(math.e) / math.sqrt(HD)


def owner_of(head, heads, n):
    low = lax.div(head * n, heads)
    odd = lax.rem(lax.div(low, 2 * inner_chips(n)), 2)
    return lax.div(head * n + odd * (heads - 1), heads)


def owned_by(index, heads, n):
    low = lax.div(index * heads, n)
    high = lax.div(index * heads + n - 1, n)
    is_low = owner_of(low, heads, n) == index
    is_high = (high < heads) & (owner_of(high, heads, n) == index)
    return is_low | is_high, jnp.where(is_low, low, high)


def inner_chips(n):
    inner = 1
    while (2 * inner) ** 2 <= n // 2:
        inner *= 2
    return inner


def greet_seq(n, me, tensor):
    barrier = pltpu.get_barrier_semaphore()

    def signal(step, carry):
        peer = (me + step) % n
        pl.semaphore_signal(barrier, inc=1, device_id=(peer, tensor), device_id_type=MESH)
        return carry

    lax.fori_loop(1, n, signal, 0)
    return barrier


def scatter_heads(
    n, heads, wide, q, k, v, ck, cv, w, out, w_out, send_sem, recv_sem, w_send, w_recv
):
    me, tensor = lax.axis_index("seq"), lax.axis_index("tensor")
    inner = inner_chips(n)
    outer = n // 2 // inner
    a, b, c = lax.div(me, 2 * inner), lax.rem(lax.div(me, 2), inner), lax.rem(me, 2)
    w_rows = w.shape[0] // CHUNKS
    barrier = greet_seq(n, me, tensor)
    pl.semaphore_wait(barrier, n - 1)
    mine, _ = owned_by(me, heads, n)

    def index(a_at, b_at, c_at):
        return (a_at * inner + b_at) * 2 + c_at

    def own(t):
        return w.at[pl.ds(t * w_rows, w_rows), pl.ds(0, wide)]

    def slot(i):
        return w_out.at[pl.ds(pl.multiple_of(i * w_rows, w_rows), w_rows)]

    def pass_block(src, i, kind, target):
        pltpu.make_async_remote_copy(
            src_ref=src,
            dst_ref=slot(i),
            send_sem=w_send.at[kind, i],
            recv_sem=w_recv.at[i],
            device_id=(target, tensor),
            device_id_type=MESH,
        ).start()

    def arrived(i):
        pltpu.make_async_copy(slot(i), slot(i), w_recv.at[i]).wait()

    def along_outer(src, i, up, down):
        if up:
            pl.when(a + 1 < outer)(lambda: pass_block(src, i, 0, index(a + 1, b, c)))
        if down:
            pl.when(a > 0)(lambda: pass_block(src, i, 1, index(a - 1, b, c)))

    def along_inner(src, i, up, down):
        if up:
            pl.when(b + 1 < inner)(lambda: pass_block(src, i, 2, index(a, b + 1, c)))
        if down:
            pl.when(b > 0)(lambda: pass_block(src, i, 3, index(a, b - 1, c)))

    def across(src, i):
        pass_block(src, i, 4, index(a, b, 1 - c))

    for t in range(CHUNKS):
        along_outer(own(t), me * CHUNKS + t, True, True)
        along_inner(own(t), me * CHUNKS + t, True, True)
    for t in range(CHUNKS):
        across(own(t), me * CHUNKS + t)
        pltpu.make_async_copy(
            own(t), slot(me * CHUNKS + t), w_recv.at[me * CHUNKS + t]
        ).start()

    def send(step, carry):
        head = lax.rem(step + me, heads)
        owner = owner_of(head, heads, n)
        columns = pl.ds(pl.multiple_of(head * HD, HD), HD)

        @pl.when(owner == me)
        def _():
            for i, ref in enumerate((q, k, v, ck, cv)):
                pltpu.make_async_copy(ref.at[:, columns], out.at[i, me], recv_sem.at[i]).start()

        @pl.when(owner != me)
        def _():
            for i, ref in enumerate((q, k, v, ck, cv)):
                pltpu.make_async_remote_copy(
                    src_ref=ref.at[:, columns],
                    dst_ref=out.at[i, me],
                    send_sem=send_sem.at[i],
                    recv_sem=recv_sem.at[i],
                    device_id=(owner, tensor),
                    device_id_type=MESH,
                ).start()

        return carry

    stages = [heads * (d + 1) // outer for d in range(outer)]
    lax.fori_loop(0, stages[0], send, 0)
    for d in range(1, outer):

        def outer_step(t, carry):
            @pl.when(a - d >= 0)
            def _():
                i = index(a - d, b, c) * CHUNKS + t
                arrived(i)
                along_outer(slot(i), i, True, False)
                along_inner(slot(i), i, True, True)
                across(slot(i), i)

            @pl.when(a + d < outer)
            def _():
                i = index(a + d, b, c) * CHUNKS + t
                arrived(i)
                along_outer(slot(i), i, False, True)
                along_inner(slot(i), i, True, True)
                across(slot(i), i)

            return carry

        lax.fori_loop(0, CHUNKS, outer_step, 0)
        lax.fori_loop(stages[d - 1], stages[d], send, 0)

    for e in range(1, inner):

        def inner_step(step, carry):
            a_at, t = lax.rem(a + lax.div(step, CHUNKS), outer), lax.rem(step, CHUNKS)

            @pl.when(b - e >= 0)
            def _():
                i = index(a_at, b - e, c) * CHUNKS + t
                arrived(i)
                along_inner(slot(i), i, True, False)
                across(slot(i), i)

            @pl.when(b + e < inner)
            def _():
                i = index(a_at, b + e, c) * CHUNKS + t
                arrived(i)
                along_inner(slot(i), i, False, True)
                across(slot(i), i)

            return carry

        lax.fori_loop(0, outer * CHUNKS, inner_step, 0)

    def sibling_step(step, carry):
        chip, t = lax.div(step, CHUNKS), lax.rem(step, CHUNKS)
        arrived((chip * 2 + (1 - c)) * CHUNKS + t)
        return carry

    lax.fori_loop(0, n // 2 * CHUNKS, sibling_step, 0)
    for t in range(CHUNKS):
        arrived(me * CHUNKS + t)

    def sent_step(step, carry):
        chip, t = lax.div(step, CHUNKS), lax.rem(step, CHUNKS)
        i = (chip * 2 + c) * CHUNKS + t
        a_at, b_at = lax.div(chip, inner), lax.rem(chip, inner)

        def sent(kind):
            pltpu.make_async_copy(slot(i), slot(i), w_send.at[kind, i]).wait()

        pl.when((b_at == b) & (a_at <= a) & (a + 1 < outer))(lambda: sent(0))
        pl.when((b_at == b) & (a_at >= a) & (a > 0))(lambda: sent(1))
        pl.when((b_at <= b) & (b + 1 < inner))(lambda: sent(2))
        pl.when((b_at >= b) & (b > 0))(lambda: sent(3))
        sent(4)
        return carry

    lax.fori_loop(0, n // 2 * CHUNKS, sent_step, 0)

    @pl.when(mine)
    def _():
        for i, ref in enumerate((q, k, v, ck, cv)):
            pltpu.make_async_copy(out.at[i], out.at[i], recv_sem.at[i]).wait()
            if heads > 1:
                part = ref.at[:, pl.ds(0, (heads - 1) * HD)]
                pltpu.make_async_copy(part, part, send_sem.at[i]).wait()

    @pl.when(jnp.logical_not(mine))
    def _():
        for i, ref in enumerate((q, k, v, ck, cv)):
            pltpu.make_async_copy(ref, ref, send_sem.at[i]).wait()


def attend_head(n, heads, rows, window, clips, slots, lengths, page_table, page_count, r, out, scores):
    contract = (((1,), (1,)), ((), ()))

    def item(c, block, start, end, base, token_blocks, page_pairs):
        query = r[0, block]
        chunks = []
        for j in range(token_blocks):
            position = (base + j) * rows + lax.broadcasted_iota(jnp.int32, (1, rows), 1)
            ok = (position >= start) & (position < end)
            chunks.append((r[1, base + j], r[2, base + j], ok))
        count = page_count[c]
        lane = lax.broadcasted_iota(jnp.int32, (1, 2 * PAGE), 1)
        for pair in range(page_pairs):
            keys, values, live = [], [], []
            for slot in (2 * pair, 2 * pair + 1):
                real = min(slot, slots - 1)
                page = page_table[c, real]
                alive = jnp.int32(slot) < count
                if slot >= slots:
                    alive = alive & False
                for before in range(real):
                    alive = alive & (page_table[c, before] != page)
                owner = page // POOL
                offset = pl.ds(pl.multiple_of((page % POOL) * PAGE, PAGE), PAGE)
                keys.append(r[3, owner, offset])
                values.append(r[4, owner, offset])
                live.append(alive.astype(jnp.int32))
            ok = jnp.where(lane < PAGE, live[0], live[1]) > 0
            chunks.append(
                (jnp.concatenate(keys, axis=0), jnp.concatenate(values, axis=0), ok)
            )
        top = None
        width = chunks[0][0].shape[0]
        for j, (key, _, ok) in enumerate(chunks):
            s = lax.dot_general(query, key, contract, preferred_element_type=jnp.float32)
            s = s * SCALE + jnp.where(ok, 0.0, -1e30)
            scores[:, j * width : (j + 1) * width] = s
            part = jnp.maximum(s[:, :HD], s[:, HD:])
            top = part if top is None else jnp.maximum(top, part)
        top = jnp.max(top, axis=1, keepdims=True)
        total = None
        for j, (_, value, _) in enumerate(chunks):
            weight = jnp.exp2(scores[:, j * width : (j + 1) * width] - top).astype(jnp.bfloat16)
            wide = jnp.concatenate([value, jnp.ones_like(value)], axis=1)
            add = jnp.dot(weight, wide, preferred_element_type=jnp.float32)
            total = add if total is None else total + add
        result = (total[:, :HD] / total[:, HD:]).astype(jnp.bfloat16)
        position = block * rows + lax.broadcasted_iota(jnp.int32, (rows, HD), 0)
        inside = (position >= start) & (position < end)
        out[block] = jnp.where(inside, result, out[block])

    mine, _ = owned_by(lax.axis_index("seq"), heads, n)

    @pl.when(mine)
    def _():
        def clip_step(c, start):
            end = start + lengths[c]
            first = start // rows
            last = (end - 1) // rows
            span = last - first + 1
            count = page_count[c]
            def run(token_blocks, page_pairs):
                base = jnp.minimum(first, n - token_blocks)

                def step(block, carry):
                    item(c, block, start, end, base, token_blocks, page_pairs)
                    return carry

                lax.fori_loop(first, last + 1, step, 0)

            sizes = [size for size in (3, 5, 6) if size < window] + [window]
            for below, token_blocks in zip([0] + sizes, sizes):
                fits = (span > below) & (span <= token_blocks)
                for page_pairs in range((slots + 1) // 2 + 1):
                    named = (count > 2 * page_pairs - 2) & (count <= 2 * page_pairs)
                    pl.when(fits & named)(functools.partial(run, token_blocks, page_pairs))
            return end

        lax.fori_loop(0, clips, clip_step, jnp.int32(0))


def return_heads(n, tensors, heads, att, out, send_sem, recv_sem, pass_sem, land_sem):
    me, tensor = lax.axis_index("seq"), lax.axis_index("tensor")
    barrier = greet_seq(n, me, tensor)

    def greet(step, carry):
        peer = (tensor + step) % tensors
        pl.semaphore_signal(barrier, inc=1, device_id=(me, peer), device_id_type=MESH)
        return carry

    lax.fori_loop(1, tensors, greet, 0)
    pl.semaphore_wait(barrier, n - 1 + tensors - 1)
    mine, my_head = owned_by(me, heads, n)

    def place(head, side):
        return out.at[:, pl.ds(pl.multiple_of((side * heads + head) * HD, HD), HD)]

    @pl.when(mine)
    def _():
        def send(step, carry):
            peer = (me + step) % n
            pltpu.make_async_remote_copy(
                src_ref=att.at[peer],
                dst_ref=place(my_head, tensor),
                send_sem=send_sem.at[0],
                recv_sem=recv_sem.at[my_head],
                device_id=(peer, tensor),
                device_id_type=MESH,
            ).start()
            return carry

        lax.fori_loop(1, n, send, 0)
        pltpu.make_async_copy(att.at[me], place(my_head, tensor), recv_sem.at[my_head]).start()

    def relay(step, carry):
        head = step
        here = place(head, tensor)
        pltpu.make_async_copy(here, here, recv_sem.at[head]).wait()

        def pass_on(other, inner):
            peer = (tensor + other) % tensors
            pltpu.make_async_remote_copy(
                src_ref=here,
                dst_ref=here,
                send_sem=pass_sem.at[head],
                recv_sem=land_sem.at[tensor, head],
                device_id=(me, peer),
                device_id_type=MESH,
            ).start()
            return inner

        lax.fori_loop(1, tensors, pass_on, 0)
        return carry

    lax.fori_loop(0, heads, relay, 0)

    def finish(step, carry):
        def land(other, inner):
            peer = (tensor + other) % tensors
            there = place(step, peer)
            pltpu.make_async_copy(there, there, land_sem.at[peer, step]).wait()
            mine_here = place(step, tensor)
            pltpu.make_async_copy(mine_here, mine_here, pass_sem.at[step]).wait()
            return inner

        return lax.fori_loop(1, tensors, land, carry)

    lax.fori_loop(0, heads, finish, 0)

    @pl.when(mine)
    def _():
        part = att.at[pl.ds(0, n - 1)]
        pltpu.make_async_copy(part, part, send_sem.at[0]).wait()


def project_rows(
    clips, rows, first_tiles, lengths, timestep, attention, w_first, w_rest, hidden, *refs
):
    gates, out = refs[:clips], refs[clips]
    tile = pl.program_id(0)
    position = lax.axis_index("seq") * rows + lax.broadcasted_iota(jnp.int32, out.shape, 0)
    gate, end = None, jnp.int32(0)
    for c in range(clips):
        row = gates[c][pl.ds(lax.rem(timestep[c], 8), 1), :]
        gate = jnp.broadcast_to(row, out.shape) if gate is None else jnp.where(position >= end, row, gate)
        end = end + lengths[c]

    def finish(weight):
        projected = jnp.dot(attention[...], weight[...], preferred_element_type=jnp.float32)
        out[...] = (hidden[...].astype(jnp.float32) + gate * projected).astype(out.dtype)

    pl.when(tile < first_tiles)(lambda: finish(w_first))
    pl.when(tile >= first_tiles)(lambda: finish(w_rest))


def local(
    n,
    tensors,
    queries,
    key_tiles,
    value_tiles,
    cache_keys,
    cache_values,
    hidden,
    out_weight,
    gate_table,
    lengths,
    page_table,
    page_count,
    timestep,
):
    rows, tile_width = queries.shape
    heads = tile_width // HD
    clips, slots = page_table.shape
    window = min(REACH + 1, n)
    pairs = (slots + 1) // 2

    width = out_weight.shape[1]
    tile = width // 5
    first_tiles = 4
    wide = first_tiles * tile

    received, w_first = pl.pallas_call(
        functools.partial(scatter_heads, n, heads, wide),
        out_shape=(
            jax.ShapeDtypeStruct((5, n, rows, HD), jnp.bfloat16),
            jax.ShapeDtypeStruct((n * out_weight.shape[0], wide), jnp.bfloat16),
        ),
        in_specs=[ANY] * 6,
        out_specs=(ANY, ANY),
        scratch_shapes=[
            pltpu.SemaphoreType.DMA((5,)),
            pltpu.SemaphoreType.DMA((5,)),
            pltpu.SemaphoreType.DMA((5, n * CHUNKS)),
            pltpu.SemaphoreType.DMA((n * CHUNKS,)),
        ],
        compiler_params=pltpu.CompilerParams(collective_id=0, has_side_effects=True),
        cost_estimate=pl.CostEstimate(flops=0, bytes_accessed=300_000_000, transcendentals=0),
        name="scatter_heads",
    )(
        queries,
        key_tiles,
        value_tiles,
        cache_keys.reshape(rows, tile_width),
        cache_values.reshape(rows, tile_width),
        out_weight,
    )
    rest, received = lax.optimization_barrier((out_weight[:, wide:], received))
    w_rest = lax.all_gather(rest, "seq", axis=0, tiled=True)

    attended = pl.pallas_call(
        functools.partial(attend_head, n, heads, rows, window, clips, slots),
        out_shape=jax.ShapeDtypeStruct((n, rows, HD), jnp.bfloat16),
        in_specs=[SMEM] * 3 + [VMEM],
        out_specs=VMEM,
        scratch_shapes=[pltpu.VMEM((rows, (window + pairs) * rows), jnp.float32)],
        compiler_params=pltpu.CompilerParams(vmem_limit_bytes=56 * 1024 * 1024),
        cost_estimate=pl.CostEstimate(
            flops=4 * n * rows * window * rows * HD,
            bytes_accessed=6 * n * rows * HD * 2,
            transcendentals=n * rows * window * rows,
        ),
        name="attend_head",
    )(lengths, page_table, page_count, received)

    attention = pl.pallas_call(
        functools.partial(return_heads, n, tensors, heads),
        out_shape=jax.ShapeDtypeStruct((rows, tensors * tile_width), jnp.bfloat16),
        in_specs=[ANY],
        out_specs=ANY,
        scratch_shapes=[
            pltpu.SemaphoreType.DMA((1,)),
            pltpu.SemaphoreType.DMA((heads,)),
            pltpu.SemaphoreType.DMA((heads,)),
            pltpu.SemaphoreType.DMA((tensors, heads)),
        ],
        compiler_params=pltpu.CompilerParams(collective_id=1, has_side_effects=True),
        cost_estimate=pl.CostEstimate(flops=0, bytes_accessed=80_000_000, transcendentals=0),
        name="return_heads",
    )(attended)

    features = n * out_weight.shape[0]
    gate_specs = [
        pl.BlockSpec((8, tile), lambda j, lengths, timestep, c=c: (lax.div(timestep[c], 8), j))
        for c in range(clips)
    ]
    return pl.pallas_call(
        functools.partial(project_rows, clips, rows, first_tiles),
        out_shape=jax.ShapeDtypeStruct(hidden.shape, hidden.dtype),
        grid_spec=pltpu.PrefetchScalarGridSpec(
            num_scalar_prefetch=2,
            grid=(width // tile,),
            in_specs=[
                pl.BlockSpec((rows, features), lambda j, *_: (0, 0)),
                pl.BlockSpec((features, tile), lambda j, *_: (0, jnp.minimum(j, first_tiles - 1))),
                pl.BlockSpec((features, tile), lambda j, *_: (0, jnp.maximum(j - first_tiles, 0))),
                pl.BlockSpec((rows, tile), lambda j, *_: (0, j)),
                *gate_specs,
            ],
            out_specs=pl.BlockSpec((rows, tile), lambda j, *_: (0, j)),
        ),
        compiler_params=pltpu.CompilerParams(vmem_limit_bytes=56 * 1024 * 1024),
        cost_estimate=pl.CostEstimate(
            flops=2 * rows * features * width,
            bytes_accessed=2 * features * width,
            transcendentals=0,
        ),
        name="project_rows",
    )(lengths, timestep, attention, w_first, w_rest, hidden, *([gate_table] * clips))


def solution(mesh):
    return jax.shard_map(
        functools.partial(local, mesh.shape["seq"], mesh.shape["tensor"]),
        mesh=mesh,
        in_specs=(
            P("seq", "tensor"),
            P("seq", "tensor"),
            P("seq", "tensor"),
            P("seq", None, "tensor"),
            P("seq", None, "tensor"),
            P("seq", "tensor"),
            P("seq", "tensor"),
            P(None, "tensor"),
            P(),
            P(),
            P(),
            P(),
        ),
        out_specs=P("seq", "tensor"),
        check_vma=False,
    )
```

```python
import functools
import math

import jax
import jax.numpy as jnp
from jax import lax
from jax.experimental import pallas as pl
from jax.experimental.pallas import tpu as pltpu
from jax.sharding import PartitionSpec as P

HD = 128
PAGE = 128
POOL = 2
REACH = 6
CHUNKS = 3

MESH = pl.DeviceIdType.MESH
ANY = pl.BlockSpec(memory_space=pl.ANY)
VMEM = pl.BlockSpec(memory_space=pltpu.VMEM)
SMEM = pl.BlockSpec(memory_space=pltpu.SMEM)
SCALE = math.log2(math.e) / math.sqrt(HD)


def owner_of(head, heads, n):
    low = lax.div(head * n, heads)
    odd = lax.rem(lax.div(low, 2 * inner_chips(n)), 2)
    return lax.div(head * n + odd * (heads - 1), heads)


def owned_by(index, heads, n):
    low = lax.div(index * heads, n)
    high = lax.div(index * heads + n - 1, n)
    is_low = owner_of(low, heads, n) == index
    is_high = (high < heads) & (owner_of(high, heads, n) == index)
    return is_low | is_high, jnp.where(is_low, low, high)


def inner_chips(n):
    inner = 1
    while (2 * inner) ** 2 <= n // 2:
        inner *= 2
    return inner


def greet_seq(n, me, tensor):
    barrier = pltpu.get_barrier_semaphore()

    def signal(step, carry):
        peer = (me + step) % n
        pl.semaphore_signal(barrier, inc=1, device_id=(peer, tensor), device_id_type=MESH)
        return carry

    lax.fori_loop(1, n, signal, 0)
    return barrier


def scatter_heads(
    n, heads, wide, q, k, v, ck, cv, w, out, w_out, send_sem, recv_sem, w_send, w_recv
):
    me, tensor = lax.axis_index("seq"), lax.axis_index("tensor")
    inner = inner_chips(n)
    outer = n // 2 // inner
    a, b, c = lax.div(me, 2 * inner), lax.rem(lax.div(me, 2), inner), lax.rem(me, 2)
    w_rows = w.shape[0] // CHUNKS
    barrier = greet_seq(n, me, tensor)
    pl.semaphore_wait(barrier, n - 1)
    mine, _ = owned_by(me, heads, n)

    def index(a_at, b_at, c_at):
        return (a_at * inner + b_at) * 2 + c_at

    def own(t):
        return w.at[pl.ds(t * w_rows, w_rows), pl.ds(0, wide)]

    def slot(i):
        return w_out.at[pl.ds(pl.multiple_of(i * w_rows, w_rows), w_rows)]

    def pass_block(src, i, kind, target):
        pltpu.make_async_remote_copy(
            src_ref=src,
            dst_ref=slot(i),
            send_sem=w_send.at[kind, i],
            recv_sem=w_recv.at[i],
            device_id=(target, tensor),
            device_id_type=MESH,
        ).start()

    def arrived(i):
        pltpu.make_async_copy(slot(i), slot(i), w_recv.at[i]).wait()

    def along_outer(src, i, up, down):
        if up:
            pl.when(a + 1 < outer)(lambda: pass_block(src, i, 0, index(a + 1, b, c)))
        if down:
            pl.when(a > 0)(lambda: pass_block(src, i, 1, index(a - 1, b, c)))

    def along_inner(src, i, up, down):
        if up:
            pl.when(b + 1 < inner)(lambda: pass_block(src, i, 2, index(a, b + 1, c)))
        if down:
            pl.when(b > 0)(lambda: pass_block(src, i, 3, index(a, b - 1, c)))

    def across(src, i):
        pass_block(src, i, 4, index(a, b, 1 - c))

    for t in range(CHUNKS):
        along_outer(own(t), me * CHUNKS + t, True, True)
        along_inner(own(t), me * CHUNKS + t, True, True)
    for t in range(CHUNKS):
        across(own(t), me * CHUNKS + t)
        pltpu.make_async_copy(
            own(t), slot(me * CHUNKS + t), w_recv.at[me * CHUNKS + t]
        ).start()

    def send(step, carry):
        head = lax.rem(step + me, heads)
        owner = owner_of(head, heads, n)
        columns = pl.ds(pl.multiple_of(head * HD, HD), HD)

        @pl.when(owner == me)
        def _():
            for i, ref in enumerate((q, k, v, ck, cv)):
                pltpu.make_async_copy(ref.at[:, columns], out.at[i, me], recv_sem.at[i]).start()

        @pl.when(owner != me)
        def _():
            for i, ref in enumerate((q, k, v, ck, cv)):
                pltpu.make_async_remote_copy(
                    src_ref=ref.at[:, columns],
                    dst_ref=out.at[i, me],
                    send_sem=send_sem.at[i],
                    recv_sem=recv_sem.at[i],
                    device_id=(owner, tensor),
                    device_id_type=MESH,
                ).start()

        return carry

    stages = [heads * (d + 1) // outer for d in range(outer)]
    lax.fori_loop(0, stages[0], send, 0)
    for d in range(1, outer):

        def outer_step(t, carry):
            @pl.when(a - d >= 0)
            def _():
                i = index(a - d, b, c) * CHUNKS + t
                arrived(i)
                along_outer(slot(i), i, True, False)
                along_inner(slot(i), i, True, True)
                across(slot(i), i)

            @pl.when(a + d < outer)
            def _():
                i = index(a + d, b, c) * CHUNKS + t
                arrived(i)
                along_outer(slot(i), i, False, True)
                along_inner(slot(i), i, True, True)
                across(slot(i), i)

            return carry

        lax.fori_loop(0, CHUNKS, outer_step, 0)
        lax.fori_loop(stages[d - 1], stages[d], send, 0)

    for e in range(1, inner):

        def inner_step(step, carry):
            a_at, t = lax.rem(a + lax.div(step, CHUNKS), outer), lax.rem(step, CHUNKS)

            @pl.when(b - e >= 0)
            def _():
                i = index(a_at, b - e, c) * CHUNKS + t
                arrived(i)
                along_inner(slot(i), i, True, False)
                across(slot(i), i)

            @pl.when(b + e < inner)
            def _():
                i = index(a_at, b + e, c) * CHUNKS + t
                arrived(i)
                along_inner(slot(i), i, False, True)
                across(slot(i), i)

            return carry

        lax.fori_loop(0, outer * CHUNKS, inner_step, 0)

    def sibling_step(step, carry):
        chip, t = lax.div(step, CHUNKS), lax.rem(step, CHUNKS)
        arrived((chip * 2 + (1 - c)) * CHUNKS + t)
        return carry

    lax.fori_loop(0, n // 2 * CHUNKS, sibling_step, 0)
    for t in range(CHUNKS):
        arrived(me * CHUNKS + t)

    def sent_step(step, carry):
        chip, t = lax.div(step, CHUNKS), lax.rem(step, CHUNKS)
        i = (chip * 2 + c) * CHUNKS + t
        a_at, b_at = lax.div(chip, inner), lax.rem(chip, inner)

        def sent(kind):
            pltpu.make_async_copy(slot(i), slot(i), w_send.at[kind, i]).wait()

        pl.when((b_at == b) & (a_at <= a) & (a + 1 < outer))(lambda: sent(0))
        pl.when((b_at == b) & (a_at >= a) & (a > 0))(lambda: sent(1))
        pl.when((b_at <= b) & (b + 1 < inner))(lambda: sent(2))
        pl.when((b_at >= b) & (b > 0))(lambda: sent(3))
        sent(4)
        return carry

    lax.fori_loop(0, n // 2 * CHUNKS, sent_step, 0)

    @pl.when(mine)
    def _():
        for i, ref in enumerate((q, k, v, ck, cv)):
            pltpu.make_async_copy(out.at[i], out.at[i], recv_sem.at[i]).wait()
            if heads > 1:
                part = ref.at[:, pl.ds(0, (heads - 1) * HD)]
                pltpu.make_async_copy(part, part, send_sem.at[i]).wait()

    @pl.when(jnp.logical_not(mine))
    def _():
        for i, ref in enumerate((q, k, v, ck, cv)):
            pltpu.make_async_copy(ref, ref, send_sem.at[i]).wait()


def attend_head(n, heads, rows, window, clips, slots, lengths, page_table, page_count, r, out, scores):
    contract = (((1,), (1,)), ((), ()))

    def item(c, block, start, end, base, token_blocks, page_pairs):
        query = r[0, block]
        chunks = []
        for j in range(token_blocks):
            position = (base + j) * rows + lax.broadcasted_iota(jnp.int32, (1, rows), 1)
            ok = (position >= start) & (position < end)
            chunks.append((r[1, base + j], r[2, base + j], ok))
        count = page_count[c]
        lane = lax.broadcasted_iota(jnp.int32, (1, 2 * PAGE), 1)
        for pair in range(page_pairs):
            keys, values, live = [], [], []
            for slot in (2 * pair, 2 * pair + 1):
                real = min(slot, slots - 1)
                page = page_table[c, real]
                alive = jnp.int32(slot) < count
                if slot >= slots:
                    alive = alive & False
                for before in range(real):
                    alive = alive & (page_table[c, before] != page)
                owner = page // POOL
                offset = pl.ds(pl.multiple_of((page % POOL) * PAGE, PAGE), PAGE)
                keys.append(r[3, owner, offset])
                values.append(r[4, owner, offset])
                live.append(alive.astype(jnp.int32))
            ok = jnp.where(lane < PAGE, live[0], live[1]) > 0
            chunks.append(
                (jnp.concatenate(keys, axis=0), jnp.concatenate(values, axis=0), ok)
            )
        top = None
        width = chunks[0][0].shape[0]
        for j, (key, _, ok) in enumerate(chunks):
            s = lax.dot_general(query, key, contract, preferred_element_type=jnp.float32)
            s = s * SCALE + jnp.where(ok, 0.0, -1e30)
            scores[:, j * width : (j + 1) * width] = s
            part = jnp.maximum(s[:, :HD], s[:, HD:])
            top = part if top is None else jnp.maximum(top, part)
        top = jnp.max(top, axis=1, keepdims=True)
        total = None
        for j, (_, value, _) in enumerate(chunks):
            weight = jnp.exp2(scores[:, j * width : (j + 1) * width] - top).astype(jnp.bfloat16)
            wide = jnp.concatenate([value, jnp.ones_like(value)], axis=1)
            add = jnp.dot(weight, wide, preferred_element_type=jnp.float32)
            total = add if total is None else total + add
        result = (total[:, :HD] / total[:, HD:]).astype(jnp.bfloat16)
        position = block * rows + lax.broadcasted_iota(jnp.int32, (rows, HD), 0)
        inside = (position >= start) & (position < end)
        out[block] = jnp.where(inside, result, out[block])

    mine, _ = owned_by(lax.axis_index("seq"), heads, n)

    @pl.when(mine)
    def _():
        def clip_step(c, start):
            end = start + lengths[c]
            first = start // rows
            last = (end - 1) // rows
            span = last - first + 1
            count = page_count[c]
            def run(token_blocks, page_pairs):
                base = jnp.minimum(first, n - token_blocks)

                def step(block, carry):
                    item(c, block, start, end, base, token_blocks, page_pairs)
                    return carry

                lax.fori_loop(first, last + 1, step, 0)

            sizes = [size for size in (3, 5, 6) if size < window] + [window]
            for below, token_blocks in zip([0] + sizes, sizes):
                fits = (span > below) & (span <= token_blocks)
                for page_pairs in range((slots + 1) // 2 + 1):
                    named = (count > 2 * page_pairs - 2) & (count <= 2 * page_pairs)
                    pl.when(fits & named)(functools.partial(run, token_blocks, page_pairs))
            return end

        lax.fori_loop(0, clips, clip_step, jnp.int32(0))


def return_heads(n, tensors, heads, att, out, send_sem, recv_sem, pass_sem, land_sem):
    me, tensor = lax.axis_index("seq"), lax.axis_index("tensor")
    barrier = greet_seq(n, me, tensor)

    def greet(step, carry):
        peer = (tensor + step) % tensors
        pl.semaphore_signal(barrier, inc=1, device_id=(me, peer), device_id_type=MESH)
        return carry

    lax.fori_loop(1, tensors, greet, 0)
    pl.semaphore_wait(barrier, n - 1 + tensors - 1)
    mine, my_head = owned_by(me, heads, n)

    def place(head, side):
        return out.at[:, pl.ds(pl.multiple_of((side * heads + head) * HD, HD), HD)]

    @pl.when(mine)
    def _():
        def send(step, carry):
            peer = (me + step) % n
            pltpu.make_async_remote_copy(
                src_ref=att.at[peer],
                dst_ref=place(my_head, tensor),
                send_sem=send_sem.at[0],
                recv_sem=recv_sem.at[my_head],
                device_id=(peer, tensor),
                device_id_type=MESH,
            ).start()
            return carry

        lax.fori_loop(1, n, send, 0)
        pltpu.make_async_copy(att.at[me], place(my_head, tensor), recv_sem.at[my_head]).start()

    def relay(step, carry):
        head = step
        here = place(head, tensor)
        pltpu.make_async_copy(here, here, recv_sem.at[head]).wait()

        def pass_on(other, inner):
            peer = (tensor + other) % tensors
            pltpu.make_async_remote_copy(
                src_ref=here,
                dst_ref=here,
                send_sem=pass_sem.at[head],
                recv_sem=land_sem.at[tensor, head],
                device_id=(me, peer),
                device_id_type=MESH,
            ).start()
            return inner

        lax.fori_loop(1, tensors, pass_on, 0)
        return carry

    lax.fori_loop(0, heads, relay, 0)

    def finish(step, carry):
        def land(other, inner):
            peer = (tensor + other) % tensors
            there = place(step, peer)
            pltpu.make_async_copy(there, there, land_sem.at[peer, step]).wait()
            mine_here = place(step, tensor)
            pltpu.make_async_copy(mine_here, mine_here, pass_sem.at[step]).wait()
            return inner

        return lax.fori_loop(1, tensors, land, carry)

    lax.fori_loop(0, heads, finish, 0)

    @pl.when(mine)
    def _():
        part = att.at[pl.ds(0, n - 1)]
        pltpu.make_async_copy(part, part, send_sem.at[0]).wait()


def project_rows(
    clips, rows, first_tiles, lengths, timestep, attention, w_first, w_rest, hidden, *refs
):
    gates, out = refs[:clips], refs[clips]
    tile = pl.program_id(0)
    position = lax.axis_index("seq") * rows + lax.broadcasted_iota(jnp.int32, out.shape, 0)
    gate, end = None, jnp.int32(0)
    for c in range(clips):
        row = gates[c][pl.ds(lax.rem(timestep[c], 8), 1), :]
        gate = jnp.broadcast_to(row, out.shape) if gate is None else jnp.where(position >= end, row, gate)
        end = end + lengths[c]

    def finish(weight):
        projected = jnp.dot(attention[...], weight[...], preferred_element_type=jnp.float32)
        out[...] = (hidden[...].astype(jnp.float32) + gate * projected).astype(out.dtype)

    pl.when(tile < first_tiles)(lambda: finish(w_first))
    pl.when(tile >= first_tiles)(lambda: finish(w_rest))


def local(
    n,
    tensors,
    queries,
    key_tiles,
    value_tiles,
    cache_keys,
    cache_values,
    hidden,
    out_weight,
    gate_table,
    lengths,
    page_table,
    page_count,
    timestep,
):
    rows, tile_width = queries.shape
    heads = tile_width // HD
    clips, slots = page_table.shape
    window = min(REACH + 1, n)
    pairs = (slots + 1) // 2

    width = out_weight.shape[1]
    tile = width // 5
    first_tiles = 3
    wide = first_tiles * tile

    w_rest = lax.all_gather(out_weight[:, wide:], "seq", axis=0, tiled=True)

    received, w_first = pl.pallas_call(
        functools.partial(scatter_heads, n, heads, wide),
        out_shape=(
            jax.ShapeDtypeStruct((5, n, rows, HD), jnp.bfloat16),
            jax.ShapeDtypeStruct((n * out_weight.shape[0], wide), jnp.bfloat16),
        ),
        in_specs=[ANY] * 6,
        out_specs=(ANY, ANY),
        scratch_shapes=[
            pltpu.SemaphoreType.DMA((5,)),
            pltpu.SemaphoreType.DMA((5,)),
            pltpu.SemaphoreType.DMA((5, n * CHUNKS)),
            pltpu.SemaphoreType.DMA((n * CHUNKS,)),
        ],
        compiler_params=pltpu.CompilerParams(collective_id=0, has_side_effects=True),
        cost_estimate=pl.CostEstimate(flops=0, bytes_accessed=300_000_000, transcendentals=0),
        name="scatter_heads",
    )(
        queries,
        key_tiles,
        value_tiles,
        cache_keys.reshape(rows, tile_width),
        cache_values.reshape(rows, tile_width),
        out_weight,
    )
    attended = pl.pallas_call(
        functools.partial(attend_head, n, heads, rows, window, clips, slots),
        out_shape=jax.ShapeDtypeStruct((n, rows, HD), jnp.bfloat16),
        in_specs=[SMEM] * 3 + [VMEM],
        out_specs=VMEM,
        scratch_shapes=[pltpu.VMEM((rows, (window + pairs) * rows), jnp.float32)],
        compiler_params=pltpu.CompilerParams(vmem_limit_bytes=56 * 1024 * 1024),
        cost_estimate=pl.CostEstimate(
            flops=4 * n * rows * window * rows * HD,
            bytes_accessed=6 * n * rows * HD * 2,
            transcendentals=n * rows * window * rows,
        ),
        name="attend_head",
    )(lengths, page_table, page_count, received)

    attention = pl.pallas_call(
        functools.partial(return_heads, n, tensors, heads),
        out_shape=jax.ShapeDtypeStruct((rows, tensors * tile_width), jnp.bfloat16),
        in_specs=[ANY],
        out_specs=ANY,
        scratch_shapes=[
            pltpu.SemaphoreType.DMA((1,)),
            pltpu.SemaphoreType.DMA((heads,)),
            pltpu.SemaphoreType.DMA((heads,)),
            pltpu.SemaphoreType.DMA((tensors, heads)),
        ],
        compiler_params=pltpu.CompilerParams(collective_id=1, has_side_effects=True),
        cost_estimate=pl.CostEstimate(flops=0, bytes_accessed=80_000_000, transcendentals=0),
        name="return_heads",
    )(attended)

    features = n * out_weight.shape[0]
    gate_specs = [
        pl.BlockSpec((8, tile), lambda j, lengths, timestep, c=c: (lax.div(timestep[c], 8), j))
        for c in range(clips)
    ]
    return pl.pallas_call(
        functools.partial(project_rows, clips, rows, first_tiles),
        out_shape=jax.ShapeDtypeStruct(hidden.shape, hidden.dtype),
        grid_spec=pltpu.PrefetchScalarGridSpec(
            num_scalar_prefetch=2,
            grid=(width // tile,),
            in_specs=[
                pl.BlockSpec((rows, features), lambda j, *_: (0, 0)),
                pl.BlockSpec((features, tile), lambda j, *_: (0, jnp.minimum(j, first_tiles - 1))),
                pl.BlockSpec((features, tile), lambda j, *_: (0, jnp.maximum(j - first_tiles, 0))),
                pl.BlockSpec((rows, tile), lambda j, *_: (0, j)),
                *gate_specs,
            ],
            out_specs=pl.BlockSpec((rows, tile), lambda j, *_: (0, j)),
        ),
        compiler_params=pltpu.CompilerParams(vmem_limit_bytes=56 * 1024 * 1024),
        cost_estimate=pl.CostEstimate(
            flops=2 * rows * features * width,
            bytes_accessed=2 * features * width,
            transcendentals=0,
        ),
        name="project_rows",
    )(lengths, timestep, attention, w_first, w_rest, hidden, *([gate_table] * clips))


def solution(mesh):
    return jax.shard_map(
        functools.partial(local, mesh.shape["seq"], mesh.shape["tensor"]),
        mesh=mesh,
        in_specs=(
            P("seq", "tensor"),
            P("seq", "tensor"),
            P("seq", "tensor"),
            P("seq", None, "tensor"),
            P("seq", None, "tensor"),
            P("seq", "tensor"),
            P("seq", "tensor"),
            P(None, "tensor"),
            P(),
            P(),
            P(),
            P(),
        ),
        out_specs=P("seq", "tensor"),
        check_vma=False,
    )
```
